32 devices in a mesh: slot: 4 (over y, core), asset: 8 (over z, x).
Axes of the slice: x: 2, y: 2, z: 4, core: 2. Of those that a mesh axis runs over, the one named last changes fastest.
Arguments:
- slot_emb: bfloat16 [8192, 768], P(('slot', 'asset')), may hold values from -4 to 4
- asset_panel: bfloat16 [768, 8192], P('slot', 'asset'), may hold values from -4 to 4
- mult: int32 [8192], P('slot'), may hold values from 1 to 4
- caps: int32 [8192], P('asset'), may hold values from 1 to 8, as said below
Outputs:
- plan: float32 [8192, 8192], P('slot', 'asset')
The draws below stay inside these ranges and needn't reach their ends.
Inputs may be any that keep to these rules, and one draw needn't show every extreme that they name: caps are whole numbers; the last asset's cap is the largest.
All inputs are finite; a program needn't handle non-finite values.
Results may differ from the reference program's by a relative error of at most 0.0003.
Values may be sent and summed in bfloat16 or wider, within the bound.
A program may use at most 64 MiB of HBM per device.

```python
import jax
import jax.numpy as jnp
from jax import lax

EMB = 768
ITERS = 3
SLOTS = 8192
ASSETS = 8192


def base_draw(key, count, width):
    first, second = jax.random.split(key)
    base = jax.random.normal(first, (count, width), jnp.float32)
    scale = jnp.exp(jax.random.uniform(second, (count, 1), jnp.float32, jnp.log(0.5), jnp.log(1.2)))
    return jnp.clip(base * scale, -4.0, 4.0)


def draw_slot_emb(key, part):
    values = base_draw(jax.random.fold_in(key, 1), SLOTS, EMB)
    return values.astype(jnp.bfloat16)


def draw_asset_panel(key, part):
    values = base_draw(jax.random.fold_in(key, 2), ASSETS, EMB)
    return values.T.astype(jnp.bfloat16)


def draw_caps(key, part):
    index = jnp.arange(ASSETS, dtype=jnp.int32)
    upper = 2 + 8 * index // ASSETS
    values = jax.random.randint(jax.random.fold_in(key, 3), (ASSETS,), 1, upper)
    return values.at[ASSETS - 1].set(8).astype(jnp.int32)


def plant(drawn, rng, least, top_value):
    longest = drawn.shape.index(max(drawn.shape))
    spots = []
    for shift in (0, 1):
        where = [jax.random.randint(jax.random.fold_in(rng, axis), (), 0, length) for axis, length in enumerate(drawn.shape)]
        where[longest] = (where[longest] + shift) % drawn.shape[longest]
        spots.append(tuple(where))
    return drawn.at[spots[0]].set(least).at[spots[1]].set(top_value)


def setup_inputs(seed: int = 0) -> dict:
    seeds = jax.random.split(jax.random.key(seed), 5)
    slot_emb = draw_slot_emb(jax.random.fold_in(seeds[4], 71), 0)
    asset_panel = draw_asset_panel(jax.random.fold_in(seeds[4], 71), 0)
    mult = plant(jax.random.randint(seeds[2], (SLOTS,), 1, 5), jax.random.fold_in(seeds[2], 1), 1, 4).astype(jnp.int32)
    caps = draw_caps(jax.random.fold_in(seeds[4], 71), 0)
    return dict(slot_emb=slot_emb, asset_panel=asset_panel, mult=mult, caps=caps)


block_count = 16


def row_lse(logits, asset_pot):
    blocks = logits.reshape(block_count, -1, logits.shape[1])

    def one_block(block):
        return jax.nn.logsumexp(block + asset_pot[None, :], axis=1)

    return lax.map(one_block, blocks).reshape(-1)


def col_lse(logits, slot_pot):
    blocks = logits.reshape(block_count, -1, logits.shape[1])
    pots = slot_pot.reshape(block_count, -1)

    def step(carry, inputs):
        peak, total = carry
        block, pot = inputs
        shifted = block + pot[:, None]
        new_peak = jnp.maximum(peak, jnp.max(shifted, axis=0))
        total = total * jnp.exp(peak - new_peak) + jnp.sum(jnp.exp(shifted - new_peak[None, :]), axis=0)
        return (new_peak, total), None

    init = (jnp.full((logits.shape[1],), -jnp.inf, jnp.float32), jnp.zeros((logits.shape[1],), jnp.float32))
    (peak, total), unused = lax.scan(step, init, (blocks, pots))
    return peak + jnp.log(total)


def reference(slot_emb, asset_panel, mult, caps):
    logits = jnp.dot(slot_emb, asset_panel, preferred_element_type=jnp.float32) * (EMB ** -0.5)
    caps_float = caps.astype(jnp.float32)
    log_b = jnp.log(caps_float) - jnp.log(jnp.sum(caps_float))
    log_a = jnp.log(mult.astype(jnp.float32))
    asset_pot = jnp.zeros((ASSETS,), jnp.float32)
    slot_pot = jnp.zeros((SLOTS,), jnp.float32)
    for iteration in range(ITERS):
        slot_pot = log_a - row_lse(logits, asset_pot)
        asset_pot = log_b - col_lse(logits, slot_pot)
    blocks = logits.reshape(block_count, -1, ASSETS)
    pots = slot_pot.reshape(block_count, -1)
    factor = float(SLOTS * ASSETS)

    def finish(inputs):
        block, pot = inputs
        return jnp.exp(block + pot[:, None] + asset_pot[None, :]) * factor

    return lax.map(finish, (blocks, pots)).reshape(SLOTS, ASSETS)
```

```python
import functools

import jax
import jax.numpy as jnp
from jax import lax
from jax.experimental import pallas as pl
from jax.experimental.pallas import tpu as pltpu
from jax.sharding import PartitionSpec as P

EMB = 768
ITERS = 3
LANES = 128
MESH = pl.DeviceIdType.MESH


def ring_spot(index, n):
    side = lax.rem(index, 2)
    up = lax.div(index, 2)
    return (1 - side) * up + side * (n - 1 - up)


def ring_index(spot, n):
    side = lax.div(spot, n // 2)
    return (1 - side) * (2 * spot) + side * (2 * (n - 1 - spot) + 1)


def loop(count, body, start=0):
    def step(i, carry):
        body(i)
        return carry

    lax.fori_loop(start, count, step, 0)


def kernel(ns, na, x_ref, w_ref, mult_ref, caps_ref, out_ref, sp_ref, ap_ref,
           xg, wg, lg, peak_ref, total_ref, spread, rbuf, cbuf, kbuf,
           rs, rr, ls, lr, ws, wr, es, er, fs, fr, ks, kr, osem):
    ms, ma = lax.axis_index("slot"), lax.axis_index("asset")
    block, depth = x_ref.shape[0], w_ref.shape[0]
    half = block // 2
    rows, cols = lg.shape
    tiles = cols // LANES
    bands = rows // LANES

    barrier = pltpu.get_barrier_semaphore()
    loop(ns, lambda d: pl.semaphore_signal(
        barrier, inc=1, device_id=(lax.rem(ms + d, ns), ma), device_id_type=MESH), 1)
    loop(na, lambda d: pl.semaphore_signal(
        barrier, inc=1, device_id=(ms, lax.rem(ma + d, na)), device_id_type=MESH), 1)

    def x_rows(spot, lower):
        return pl.ds(pl.multiple_of(ring_index(spot, na) * block + lower * half, half), half)

    def w_rows(owner):
        return pl.ds(pl.multiple_of(owner * depth, depth), depth)

    here = ring_spot(ma, na)
    right = ring_index(lax.rem(here + 1, na), na)
    left = ring_index(lax.rem(here + na - 1, na), na)
    xg[pl.ds(pl.multiple_of(ma * block, block), block), :] = x_ref[...]
    wg[w_rows(ms), :] = w_ref[...]
    caps = caps_ref[...].astype(jnp.float32)
    kbuf[ma] = jnp.broadcast_to(
        jnp.sum(jnp.sum(caps, axis=0, keepdims=True), axis=1, keepdims=True), (8, LANES))
    pl.semaphore_wait(barrier, ns + na - 2)

    def to_right(s):
        part = xg.at[x_rows(lax.rem(here + na - s, na), 0), :]
        return pltpu.make_async_remote_copy(
            src_ref=part, dst_ref=part, send_sem=rs.at[s], recv_sem=rr.at[s],
            device_id=(ms, right), device_id_type=MESH)

    def to_left(s):
        part = xg.at[x_rows(lax.rem(here + s, na), 1), :]
        return pltpu.make_async_remote_copy(
            src_ref=part, dst_ref=part, send_sem=ls.at[s], recv_sem=lr.at[s],
            device_id=(ms, left), device_id_type=MESH)

    def from_left(s):
        part = xg.at[x_rows(lax.rem(here + na - s - 1, na), 0), :]
        return pltpu.make_async_remote_copy(
            src_ref=part, dst_ref=part, send_sem=rs.at[s], recv_sem=rr.at[s],
            device_id=(ms, right), device_id_type=MESH)

    def from_right(s):
        part = xg.at[x_rows(lax.rem(here + s + 1, na), 1), :]
        return pltpu.make_async_remote_copy(
            src_ref=part, dst_ref=part, send_sem=ls.at[s], recv_sem=lr.at[s],
            device_id=(ms, left), device_id_type=MESH)

    def panel(d, owner):
        part = wg.at[w_rows(owner), :]
        return pltpu.make_async_remote_copy(
            src_ref=part, dst_ref=part, send_sem=ws.at[d], recv_sem=wr.at[d],
            device_id=(lax.rem(ms + d, ns), ma), device_id_type=MESH)

    def swap(buf, send, recv, slot, n, axis_slot):
        me = ms if axis_slot else ma

        def copy(d, owner):
            peer = lax.rem(me + d, n)
            part = buf.at[(slot, owner) if slot is not None else (owner,)]
            k = (slot, d) if slot is not None else (d,)
            return pltpu.make_async_remote_copy(
                src_ref=part, dst_ref=part, send_sem=send.at[k], recv_sem=recv.at[k],
                device_id=(peer, ma) if axis_slot else (ms, peer), device_id_type=MESH)

        def start():
            loop(n, lambda d: copy(d, me).start(), 1)

        def finish():
            loop(n, lambda d: copy(d, lax.rem(me + n - d, n)).wait_recv(), 1)
            loop(n, lambda d: copy(d, me).wait_send(), 1)

        return start, finish

    def product(t):
        for spot, lower in ((lax.rem(here + na - t, na), 0), (lax.rem(here + t, na), 1)):
            part = x_rows(spot, lower)
            lg[part, :] = jnp.dot(
                xg[part, :], wg[...], preferred_element_type=jnp.float32) * EMB ** (-0.5)

    def hop(s):
        from_left(s).wait_recv()
        from_right(s).wait_recv()

        @pl.when(s + 1 < na - 1)
        def _():
            to_right(s + 1).start()
            to_left(s + 1).start()

    to_right(0).start()
    to_left(0).start()
    loop(ns, lambda d: panel(d, ms).start(), 1)
    caps_start, caps_finish = swap(kbuf, ks, kr, None, na, False)
    caps_start()

    early = na // 2
    loop(early, hop)
    loop(ns, lambda d: panel(d, lax.rem(ms + ns - d, ns)).wait_recv(), 1)

    def late(u):
        hop(early + u)
        product(2 * u)
        product(2 * u + 1)

    loop(na - 1 - early, late)
    loop(na, product, 2 * (na - 1 - early))

    out = pltpu.make_async_copy(lg, out_ref, osem)
    out.start()

    caps_finish()
    log_b = jnp.log(caps) - jnp.log(jnp.sum(kbuf[...], axis=0)[0:1, :])
    log_a = jnp.log(mult_ref[...].astype(jnp.float32))
    ap_ref[...] = jnp.zeros_like(ap_ref)

    rchunk = 32
    cchunk = 64

    def lanes(k):
        return slice(k * LANES, (k + 1) * LANES)

    def join(parts):
        peak = jnp.max(parts, axis=0)
        return peak + jnp.log(jnp.sum(jnp.exp(parts - peak[None]), axis=0))

    for it in range(ITERS):
        def row_step(i):
            r = pl.ds(pl.multiple_of(i * rchunk, rchunk), rchunk)
            shifted = [lg[r, lanes(k)] + ap_ref[k:k + 1, :] for k in range(tiles)]
            peak = functools.reduce(jnp.maximum, shifted)
            peak_ref[r, :] = peak
            total_ref[r, :] = functools.reduce(jnp.add, [jnp.exp(v - peak) for v in shifted])

        loop(rows // rchunk, row_step)
        for b in range(bands):
            peaks = peak_ref[b * LANES:(b + 1) * LANES, :].T
            totals = total_ref[b * LANES:(b + 1) * LANES, :].T
            peak = jnp.max(peaks, axis=0, keepdims=True)
            total = jnp.sum(totals * jnp.exp(peaks - peak), axis=0, keepdims=True)
            rbuf[it, ma, b:b + 1, :] = peak + jnp.log(total)
        start, finish = swap(rbuf, es, er, it, na, False)
        start()
        finish()
        sp_ref[...] = log_a - join(rbuf[it])
        for b in range(bands):
            spread[b * LANES:(b + 1) * LANES, :] = jnp.broadcast_to(
                sp_ref[b:b + 1, :], (LANES, LANES)).T

        for k in range(tiles):
            def col_step(i, carry):
                peak, total = carry
                r = pl.ds(pl.multiple_of(i * cchunk, cchunk), cchunk)
                shifted = (lg[r, lanes(k)] + spread[r, :]).reshape(cchunk // 8, 8, LANES)
                fresh = jnp.maximum(peak, jnp.max(shifted, axis=0))
                total = total * jnp.exp(peak - fresh) + jnp.sum(
                    jnp.exp(shifted - fresh[None]), axis=0)
                return fresh, total

            init = (jnp.full((8, LANES), -jnp.inf, jnp.float32), jnp.zeros((8, LANES), jnp.float32))
            peaks, totals = lax.fori_loop(0, rows // cchunk, col_step, init, unroll=2)
            peak = jnp.max(peaks, axis=0, keepdims=True)
            total = jnp.sum(totals * jnp.exp(peaks - peak), axis=0, keepdims=True)
            cbuf[it, ms, k:k + 1, :] = peak + jnp.log(total)
        start, finish = swap(cbuf, fs, fr, it, ns, True)
        start()
        finish()
        ap_ref[...] = log_b - join(cbuf[it])

    def drain(s):
        to_right(s).wait_send()
        to_left(s).wait_send()

    loop(na - 1, drain)
    loop(ns, lambda d: panel(d, ms).wait_send(), 1)
    out.wait()


def per_device(ns, na, slot_emb, asset_panel, mult, caps):
    rows, cols = mult.shape[0], caps.shape[0]
    bands, tiles = rows // LANES, cols // LANES
    vmem = pl.BlockSpec(memory_space=pltpu.VMEM)
    dma = pltpu.SemaphoreType.DMA
    f32 = jnp.float32
    logits, slot_pot, asset_pot = pl.pallas_call(
        functools.partial(kernel, ns, na),
        out_shape=(
            jax.ShapeDtypeStruct((rows, cols), f32),
            jax.ShapeDtypeStruct((bands, LANES), f32),
            jax.ShapeDtypeStruct((tiles, LANES), f32),
        ),
        in_specs=[vmem] * 4,
        out_specs=(pl.BlockSpec(memory_space=pl.ANY), vmem, vmem),
        scratch_shapes=[
            pltpu.VMEM((rows, EMB), jnp.bfloat16),
            pltpu.VMEM((EMB, cols), jnp.bfloat16),
            pltpu.VMEM((rows, cols), f32),
            pltpu.VMEM((rows, LANES), f32),
            pltpu.VMEM((rows, LANES), f32),
            pltpu.VMEM((rows, LANES), f32),
            pltpu.VMEM((ITERS, na, bands, LANES), f32),
            pltpu.VMEM((ITERS, ns, tiles, LANES), f32),
            pltpu.VMEM((na, 8, LANES), f32),
            dma((na,)), dma((na,)), dma((na,)), dma((na,)),
            dma((ns,)), dma((ns,)),
            dma((ITERS, na)), dma((ITERS, na)),
            dma((ITERS, ns)), dma((ITERS, ns)),
            dma((na,)), dma((na,)),
            dma,
        ],
        compiler_params=pltpu.CompilerParams(
            collective_id=0, has_side_effects=True, vmem_limit_bytes=40 * 2**20),
    )(slot_emb, asset_panel, mult.reshape(bands, LANES), caps.reshape(tiles, LANES))
    factor = float(rows * ns * cols * na)
    return jnp.exp(
        logits + slot_pot.reshape(rows)[:, None] + asset_pot.reshape(cols)[None, :]) * factor


def solution(mesh):
    return jax.shard_map(
        functools.partial(per_device, mesh.shape["slot"], mesh.shape["asset"]),
        mesh=mesh,
        in_specs=(P(("slot", "asset"), None), P("slot", "asset"), P("slot"), P("asset")),
        out_specs=P("slot", "asset"),
        check_vma=False,
    )
```

```python
import functools
import math

import jax
import jax.numpy as jnp
from jax import lax
from jax.experimental import pallas as pl
from jax.experimental.pallas import tpu as pltpu
from jax.sharding import PartitionSpec as P

EMB = 768
ITERS = 3
SCALE = EMB ** (-0.5) * math.log2(math.e)
LANES = 128
MESH = pl.DeviceIdType.MESH


def ring_spot(index, n):
    side = lax.rem(index, 2)
    up = lax.div(index, 2)
    return (1 - side) * up + side * (n - 1 - up)


def ring_index(spot, n):
    side = lax.div(spot, n // 2)
    return (1 - side) * (2 * spot) + side * (2 * (n - 1 - spot) + 1)


def loop(count, body, start=0):
    def step(i, carry):
        body(i)
        return carry

    lax.fori_loop(start, count, step, 0)


def kernel(ns, na, x_ref, w_ref, mult_ref, caps_ref, out_ref, sp_ref, ap_ref,
           xg, wg, lg, peak_ref, total_ref, spread, rbuf, cbuf, kbuf,
           rs, rr, ls, lr, ws, wr, es, er, fs, fr, ks, kr, osem,
           isem, caps_own, mult_own):
    ms, ma = lax.axis_index("slot"), lax.axis_index("asset")
    block, depth = x_ref.shape[0], w_ref.shape[0]
    half = block // 2
    rows, cols = lg.shape
    tiles = cols // LANES
    bands = rows // LANES

    barrier = pltpu.get_barrier_semaphore()
    loop(ns, lambda d: pl.semaphore_signal(
        barrier, inc=1, device_id=(lax.rem(ms + d, ns), ma), device_id_type=MESH), 1)
    loop(na, lambda d: pl.semaphore_signal(
        barrier, inc=1, device_id=(ms, lax.rem(ma + d, na)), device_id_type=MESH), 1)

    def x_rows(spot, lower):
        return pl.ds(pl.multiple_of(ring_index(spot, na) * block + lower * half, half), half)

    def w_rows(owner):
        return pl.ds(pl.multiple_of(owner * depth, depth), depth)

    here = ring_spot(ma, na)
    right = ring_index(lax.rem(here + 1, na), na)
    left = ring_index(lax.rem(here + na - 1, na), na)
    loads = [
        pltpu.make_async_copy(x_ref, xg.at[pl.ds(pl.multiple_of(ma * block, block), block), :], isem.at[0]),
        pltpu.make_async_copy(w_ref, wg.at[w_rows(ms), :], isem.at[1]),
        pltpu.make_async_copy(caps_ref, caps_own, isem.at[2]),
        pltpu.make_async_copy(mult_ref, mult_own, isem.at[3]),
    ]
    for load in loads:
        load.start()
    ap_ref[...] = jnp.zeros_like(ap_ref)
    for load in loads:
        load.wait()
    caps = caps_own[...].astype(jnp.float32)
    kbuf[ma] = jnp.broadcast_to(
        jnp.sum(jnp.sum(caps, axis=0, keepdims=True), axis=1, keepdims=True), (8, LANES))
    pl.semaphore_wait(barrier, ns + na - 2)

    def to_right(s):
        part = xg.at[x_rows(lax.rem(here + na - s, na), 0), :]
        return pltpu.make_async_remote_copy(
            src_ref=part, dst_ref=part, send_sem=rs.at[s], recv_sem=rr.at[s],
            device_id=(ms, right), device_id_type=MESH)

    def to_left(s):
        part = xg.at[x_rows(lax.rem(here + s, na), 1), :]
        return pltpu.make_async_remote_copy(
            src_ref=part, dst_ref=part, send_sem=ls.at[s], recv_sem=lr.at[s],
            device_id=(ms, left), device_id_type=MESH)

    def from_left(s):
        part = xg.at[x_rows(lax.rem(here + na - s - 1, na), 0), :]
        return pltpu.make_async_remote_copy(
            src_ref=part, dst_ref=part, send_sem=rs.at[s], recv_sem=rr.at[s],
            device_id=(ms, right), device_id_type=MESH)

    def from_right(s):
        part = xg.at[x_rows(lax.rem(here + s + 1, na), 1), :]
        return pltpu.make_async_remote_copy(
            src_ref=part, dst_ref=part, send_sem=ls.at[s], recv_sem=lr.at[s],
            device_id=(ms, left), device_id_type=MESH)

    def panel(d, owner):
        part = wg.at[w_rows(owner), :]
        return pltpu.make_async_remote_copy(
            src_ref=part, dst_ref=part, send_sem=ws.at[d], recv_sem=wr.at[d],
            device_id=(lax.rem(ms + d, ns), ma), device_id_type=MESH)

    sent = []

    def swap(buf, send, recv, slot, n, axis_slot):
        me = ms if axis_slot else ma

        def copy(d, owner):
            peer = lax.rem(me + d, n)
            part = buf.at[(slot, owner) if slot is not None else (owner,)]
            k = (slot, d) if slot is not None else (d,)
            return pltpu.make_async_remote_copy(
                src_ref=part, dst_ref=part, send_sem=send.at[k], recv_sem=recv.at[k],
                device_id=(peer, ma) if axis_slot else (ms, peer), device_id_type=MESH)

        def start():
            loop(n, lambda d: copy(d, me).start(), 1)

        def finish():
            loop(n, lambda d: copy(d, lax.rem(me + n - d, n)).wait_recv(), 1)
            sent.append(lambda: loop(n, lambda d: copy(d, me).wait_send(), 1))

        return start, finish

    rchunk = 32
    cchunk = 128

    def lanes(k):
        return slice(k * LANES, (k + 1) * LANES)

    def row_step(first):
        r = pl.ds(first, rchunk)
        shifted = [lg[r, lanes(k)] + ap_ref[k:k + 1, :] for k in range(tiles)]
        peak = functools.reduce(jnp.maximum, shifted)
        peak_ref[r, :] = peak
        total_ref[r, :] = functools.reduce(jnp.add, [jnp.exp2(v - peak) for v in shifted])

    def product(t):
        for spot, lower in ((lax.rem(here + na - t, na), 0), (lax.rem(here + t, na), 1)):
            part = x_rows(spot, lower)
            lg[part, :] = jnp.dot(
                xg[part, :], wg[...], preferred_element_type=jnp.float32) * SCALE
            first = ring_index(spot, na) * block + lower * half
            for j in range(half // rchunk):
                row_step(pl.multiple_of(first + j * rchunk, rchunk))

    def hop(s):
        from_left(s).wait_recv()

        @pl.when(s + 1 < na - 1)
        def _():
            to_right(s + 1).start()

        from_right(s).wait_recv()

        @pl.when(s + 1 < na - 1)
        def _():
            to_left(s + 1).start()

    to_right(0).start()
    to_left(0).start()
    loop(ns, lambda d: panel(d, ms).start(), 1)
    caps_start, caps_finish = swap(kbuf, ks, kr, None, na, False)
    caps_start()

    early = na // 2
    loop(early, hop)
    loop(ns, lambda d: panel(d, lax.rem(ms + ns - d, ns)).wait_recv(), 1)

    def late(u):
        hop(early + u)
        product(2 * u)
        product(2 * u + 1)

    loop(na - 1 - early, late)
    loop(na, product, 2 * (na - 1 - early))

    out = pltpu.make_async_copy(lg, out_ref, osem)
    out.start()

    caps_finish()
    log_b = jnp.log2(caps) - jnp.log2(jnp.sum(kbuf[...], axis=0)[0:1, :])
    log_a = jnp.log2(mult_own[...].astype(jnp.float32))

    def join(parts):
        peak = jnp.max(parts, axis=0)
        return peak + jnp.log2(jnp.sum(jnp.exp2(parts - peak[None]), axis=0))

    for it in range(ITERS):
        if it:
            def row_pair(i):
                for j in range(2):
                    row_step(pl.multiple_of((2 * i + j) * rchunk, rchunk))

            loop(rows // (2 * rchunk), row_pair)
        for b in range(bands):
            peaks = peak_ref[b * LANES:(b + 1) * LANES, :].T
            totals = total_ref[b * LANES:(b + 1) * LANES, :].T
            peak = jnp.max(peaks, axis=0, keepdims=True)
            total = jnp.sum(totals * jnp.exp2(peaks - peak), axis=0, keepdims=True)
            rbuf[it, ma, b:b + 1, :] = peak + jnp.log2(total)
        start, finish = swap(rbuf, es, er, it, na, False)
        start()
        finish()
        sp_ref[...] = log_a - join(rbuf[it])
        for b in range(bands):
            spread[b * LANES:(b + 1) * LANES, :] = jnp.broadcast_to(
                sp_ref[b:b + 1, :], (LANES, LANES)).T

        for k in range(0, tiles, 2):
            def col_step(i, carry):
                r = pl.ds(pl.multiple_of(i * cchunk, cchunk), cchunk)
                pots = spread[r, :]
                result = []
                for j, (peak, total) in enumerate(carry):
                    shifted = (lg[r, lanes(k + j)] + pots).reshape(cchunk // 8, 8, LANES)
                    fresh = jnp.maximum(peak, jnp.max(shifted, axis=0))
                    total = total * jnp.exp2(peak - fresh) + jnp.sum(
                        jnp.exp2(shifted - fresh[None]), axis=0)
                    result.append((fresh, total))
                return tuple(result)

            init = (jnp.full((8, LANES), -jnp.inf, jnp.float32), jnp.zeros((8, LANES), jnp.float32))
            done = lax.fori_loop(0, rows // cchunk, col_step, (init, init))
            for j, (peaks, totals) in enumerate(done):
                peak = jnp.max(peaks, axis=0, keepdims=True)
                total = jnp.sum(totals * jnp.exp2(peaks - peak), axis=0, keepdims=True)
                cbuf[it, ms, k + j:k + j + 1, :] = peak + jnp.log2(total)
        start, finish = swap(cbuf, fs, fr, it, ns, True)
        start()
        finish()
        ap_ref[...] = log_b - join(cbuf[it])

    def drain(s):
        to_right(s).wait_send()
        to_left(s).wait_send()

    loop(na - 1, drain)
    for wait in sent:
        wait()
    loop(ns, lambda d: panel(d, ms).wait_send(), 1)
    out.wait()


def per_device(ns, na, slot_emb, asset_panel, mult, caps):
    rows, cols = mult.shape[0], caps.shape[0]
    bands, tiles = rows // LANES, cols // LANES
    vmem = pl.BlockSpec(memory_space=pltpu.VMEM)
    dma = pltpu.SemaphoreType.DMA
    f32 = jnp.float32
    logits, slot_pot, asset_pot = pl.pallas_call(
        functools.partial(kernel, ns, na),
        out_shape=(
            jax.ShapeDtypeStruct((rows, cols), f32),
            jax.ShapeDtypeStruct((bands, LANES), f32),
            jax.ShapeDtypeStruct((tiles, LANES), f32),
        ),
        in_specs=[pl.BlockSpec(memory_space=pltpu.HBM)] * 4,
        out_specs=(pl.BlockSpec(memory_space=pl.ANY), vmem, vmem),
        scratch_shapes=[
            pltpu.VMEM((rows, EMB), jnp.bfloat16),
            pltpu.VMEM((EMB, cols), jnp.bfloat16),
            pltpu.VMEM((rows, cols), f32),
            pltpu.VMEM((rows, LANES), f32),
            pltpu.VMEM((rows, LANES), f32),
            pltpu.VMEM((rows, LANES), f32),
            pltpu.VMEM((ITERS, na, bands, LANES), f32),
            pltpu.VMEM((ITERS, ns, tiles, LANES), f32),
            pltpu.VMEM((na, 8, LANES), f32),
            dma((na,)), dma((na,)), dma((na,)), dma((na,)),
            dma((ns,)), dma((ns,)),
            dma((ITERS, na)), dma((ITERS, na)),
            dma((ITERS, ns)), dma((ITERS, ns)),
            dma((na,)), dma((na,)),
            dma,
            dma((4,)),
            pltpu.VMEM((tiles, LANES), jnp.int32),
            pltpu.VMEM((bands, LANES), jnp.int32),
        ],
        compiler_params=pltpu.CompilerParams(
            collective_id=0, has_side_effects=True, vmem_limit_bytes=40 * 2**20),
    )(slot_emb, asset_panel, mult.reshape(bands, LANES), caps.reshape(tiles, LANES))
    factor = float(rows * ns * cols * na)
    return jnp.exp2(
        logits + slot_pot.reshape(rows)[:, None] + asset_pot.reshape(cols)[None, :]) * factor


def solution(mesh):
    return jax.shard_map(
        functools.partial(per_device, mesh.shape["slot"], mesh.shape["asset"]),
        mesh=mesh,
        in_specs=(P(("slot", "asset"), None), P("slot", "asset"), P("slot"), P("asset")),
        out_specs=P("slot", "asset"),
        check_vma=False,
    )
```
